32 devices in a mesh: scene: 2 (over x), gx: 16 (over z, y, core).
Axes of the slice: x: 2, y: 2, z: 4, core: 2. Of those that a mesh axis runs over, the one named last changes fastest.
Arguments:
- cotangent: float32 [128, 128, 256], P(('scene', 'gx')), parts along dimension 0, may hold values from -24 to 24
- counts: int32 [128, 128, 256], P(('scene', 'gx')), parts along dimension 0, may hold values from 0 to 31
Outputs:
- multiplier: float32 [128, 128, 256], P(('scene', 'gx')), parts along dimension 0
- normal_grad: float32 [3, 128, 128, 256], P(None, ('scene', 'gx')), parts along dimension 1
The draws below stay inside these ranges and needn't reach their ends.
There are 2 independent parts, one for each index of `scene`. The reference program is written for one: setup_inputs(seed, part) draws one part's arguments, and reference() takes and returns one part's arrays. A program takes and returns all parts, laid end to end along the dimension named above; each array names one. Nothing has to cross between parts.
All inputs are finite; a program needn't handle non-finite values.
Results may differ from the reference program's by a relative error of at most 0.0001.
Values sent between devices are 32-bit elements; how exact they have to be, the bound alone decides.
A program may use at most 128 MiB of HBM per device.

```python
import jax
import jax.numpy as jnp

NY = 128
NZ = 256
LEVELS = 3
SWEEPS = 2
COARSE = 16
CYCLES = 2
NX = 64


def touch_ends(values, stream_key, smallest, top_value):
    spot = [jax.random.randint(jax.random.fold_in(stream_key, axis), (), 0, length) for axis, length in enumerate(values.shape)]
    longest = values.shape.index(max(values.shape))
    neighbour = spot[:longest] + [(spot[longest] + 1) % values.shape[longest]] + spot[longest + 1:]
    return values.at[tuple(spot)].set(smallest).at[tuple(neighbour)].set(top_value)


def levels(rng, dims, split, low, top_value):
    factor_of = 1.0
    for axis_at, parts in split:
        steps = jax.random.uniform(jax.random.fold_in(jax.random.fold_in(rng, 6), axis_at), (parts,), jnp.float32, low / len(split), top_value / len(split))
        factor_of = factor_of * jnp.repeat(jnp.exp(steps), dims[axis_at] // parts).reshape((-1,) + (1,) * (len(dims) - 1 - axis_at))
    return factor_of


def scatter_about(rng, shape, spread, most, pieces=(), kind=jnp.bfloat16):
    drawn = jax.random.normal(rng, shape, jnp.float32) * spread
    if len(pieces) > 0:
        drawn = levels(rng, shape, pieces, -0.22, 0.18) * drawn
    return jnp.clip(drawn, min=-most, max=most).astype(kind)


def setup_inputs(seed: int = 0, part: int = 0) -> dict:
    streams_of = jax.random.split(jax.random.key(seed), 3)
    own_keys = jax.random.split(jax.random.fold_in(streams_of[2], part), 3)
    cotangent = scatter_about(own_keys[0], (NX, NY, NZ), 4.0, 24.0, ((0, 16),), jnp.float32)
    counts = touch_ends(jax.random.randint(own_keys[1], (NX, NY, NZ), 0, 32), jax.random.fold_in(own_keys[1], 1), 0, 31).astype(jnp.int32)
    return {"cotangent": cotangent, "counts": counts}


damping = 0.8
screen_rate = 0.004


def operate(field, weight, inv_h2):
    padded = jnp.pad(field, 1)
    beside = padded[2:, 1:-1, 1:-1] + padded[:-2, 1:-1, 1:-1]
    beside = beside + padded[1:-1, 2:, 1:-1] + padded[1:-1, :-2, 1:-1]
    beside = beside + padded[1:-1, 1:-1, 2:] + padded[1:-1, 1:-1, :-2]
    return inv_h2 * (6.0 * field - beside) + weight * field


def relax_sweep(field, source, weight, inv_h2):
    return field + damping * (source - operate(field, weight, inv_h2)) / (6.0 * inv_h2 + weight)


def restrict(field):
    sx, sy, sz = field.shape
    return field.reshape(sx // 2, 2, sy // 2, 2, sz // 2, 2).mean(axis=(1, 3, 5))


def prolong(field):
    return jnp.repeat(jnp.repeat(jnp.repeat(field, 2, axis=0), 2, axis=1), 2, axis=2)


def vcycle(level_index, field, source, screens):
    weight = screens[level_index]
    inv_h2 = 0.25 ** level_index
    if level_index == LEVELS - 1:
        for _ in range(COARSE):
            field = relax_sweep(field, source, weight, inv_h2)
        return field
    for _ in range(SWEEPS):
        field = relax_sweep(field, source, weight, inv_h2)
    resid = source - operate(field, weight, inv_h2)
    coarse_rhs = restrict(resid)
    error = vcycle(level_index + 1, jnp.zeros_like(coarse_rhs), coarse_rhs, screens)
    field = field + prolong(error)
    for _ in range(SWEEPS):
        field = relax_sweep(field, source, weight, inv_h2)
    return field


def reference(cotangent, counts):
    screens = [screen_rate * counts.astype(jnp.float32)]
    for _ in range(LEVELS - 1):
        screens.append(restrict(screens[-1]))
    multiplier = jnp.zeros_like(cotangent)
    for _ in range(CYCLES):
        multiplier = vcycle(0, multiplier, cotangent, screens)
    ahead_x = jnp.pad(multiplier[1:], ((0, 1), (0, 0), (0, 0)))
    ahead_y = jnp.pad(multiplier[:, 1:], ((0, 0), (0, 1), (0, 0)))
    ahead_z = jnp.pad(multiplier[:, :, 1:], ((0, 0), (0, 0), (0, 1)))
    normal_grad = jnp.stack([multiplier - ahead_x, multiplier - ahead_y, multiplier - ahead_z])
    return multiplier, normal_grad
```

```python
import functools

import jax
import jax.numpy as jnp
from jax import lax
from jax.experimental import pallas as pl
from jax.experimental.pallas import tpu as pltpu
from jax.sharding import PartitionSpec as P

SWEEPS = 2
COARSE = 16
CYCLES = 2
DAMPING = 0.8
KEEP = 1.0 - DAMPING
RATE = 0.004
MESH = pl.DeviceIdType.MESH
PAD = 8
CHUNK = 32


def dot(a, b):
    return lax.dot(a, b, precision=lax.Precision.HIGHEST, preferred_element_type=jnp.float32)


def pick(shape, row_of, column_of):
    r = lax.broadcasted_iota(jnp.int32, shape, 0)
    c = lax.broadcasted_iota(jnp.int32, shape, 1)
    return jnp.where(row_of(r) == column_of(c), 1.0, 0.0).astype(jnp.float32)


def z_sides(x):
    last = x.shape[1] - 1
    lane = lax.broadcasted_iota(jnp.int32, x.shape, 1)
    before = jnp.where(lane == 0, 0.0, pltpu.roll(x, 1, 1))
    return before + jnp.where(lane == last, 0.0, pltpu.roll(x, last, 1))


def y_sides(x):
    last = x.shape[0] - 1
    row = lax.broadcasted_iota(jnp.int32, x.shape, 0)
    before = jnp.where(row == 0, 0.0, pltpu.roll(x, 1, 0))
    return before + jnp.where(row == last, 0.0, pltpu.roll(x, last, 0))


def kernel(n, f_ref, counts_ref, out_ref, ahead_ref, va, vb, c_ref, d_ref, halo, quarter, rs,
           cm, rm, e2, ea, eb, qown, gc, gr, xa, xb, fsend, frecv, gsend, grecv):
    me = lax.axis_index("gx")
    ny, nz = f_ref.shape[1:]
    my, mz = ny // 2, nz // 2
    cy, cz = my // 4, mz
    rows = pl.ds(PAD, ny)

    for ref in (va, vb):
        for p in range(ref.shape[0]):
            ref[p, pl.ds(0, PAD), :] = jnp.zeros((PAD, nz), jnp.float32)
            ref[p, pl.ds(PAD + ny, PAD), :] = jnp.zeros((PAD, nz), jnp.float32)
    cm[...] = jnp.zeros_like(cm)
    rm[...] = jnp.zeros_like(rm)
    e2[...] = jnp.zeros_like(e2)
    for ref in (xa, xb):
        for p in (0, 1, n + 2, n + 3):
            ref[p] = jnp.zeros((cy, cz), jnp.float32)

    @pl.when(me == 0)
    def _():
        for k in range(halo.shape[0]):
            halo[k, 0] = jnp.zeros((ny, nz), jnp.float32)
        for k in range(CYCLES):
            quarter[k, 0] = jnp.zeros((my, mz), jnp.float32)

    @pl.when(me == n - 1)
    def _():
        for k in range(halo.shape[0]):
            halo[k, 1] = jnp.zeros((ny, nz), jnp.float32)
        for k in range(CYCLES):
            quarter[k, 1] = jnp.zeros((my, mz), jnp.float32)

    barrier = pltpu.get_barrier_semaphore()

    def greet(k, _):
        pl.semaphore_signal(barrier, inc=1, device_id={"gx": lax.rem(me + k, n)}, device_id_type=MESH)
        return 0

    lax.fori_loop(1, n, greet, 0)

    used = [0]

    class Transfer:
        def __init__(self, src, dst, dist):
            self.dist, self.src, self.dst, self.j = dist, src, dst, used[0]
            used[0] += 1

        def copy(self):
            return pltpu.make_async_remote_copy(
                src_ref=self.src, dst_ref=self.dst, send_sem=fsend.at[self.j],
                recv_sem=frecv.at[self.j], device_id={"gx": me + self.dist}, device_id_type=MESH)

        def inside(self, sign):
            return me < n - self.dist * sign if self.dist * sign > 0 else me >= -self.dist * sign

        def start(self):
            @pl.when(self.inside(1))
            def _():
                self.copy().start()
            return self

        def arrived(self):
            @pl.when(self.inside(-1))
            def _():
                self.copy().wait_recv()

        def sent(self):
            @pl.when(self.inside(1))
            def _():
                self.copy().wait_send()

        def wait(self):
            self.arrived()
            self.sent()

    def gather_copy(g, ref, k, peer, owner):
        return pltpu.make_async_remote_copy(
            src_ref=ref.at[owner], dst_ref=ref.at[owner], send_sem=gsend.at[g, k],
            recv_sem=grecv.at[g, k], device_id={"gx": peer}, device_id_type=MESH)

    def gather_start(g, ref):
        def body(k, _):
            gather_copy(g, ref, k, lax.rem(me + k, n), me).start()
            return 0
        lax.fori_loop(1, n, body, 0)

    def gather_wait(g, ref):
        def body(k, _):
            c = gather_copy(g, ref, k, lax.rem(me + k, n), lax.rem(me + n - k, n))
            c.wait_recv()
            c.wait_send()
            return 0
        lax.fori_loop(1, n, body, 0)

    def halves(r, c):
        return r // 2, c // 2

    ry_f = pick((my, ny), lambda r: r, lambda c: c // 2)
    rz_f = pick((nz, mz), lambda r: r // 2, lambda c: c)
    py_f = pick((ny, my), lambda r: r // 2, lambda c: c)
    pz_f = pick((mz, nz), lambda r: r, lambda c: c // 2)
    half = mz // 2
    ry_m = [pick((cy, my), lambda r, o=o: 2 * r + o, lambda c: c // 2) for o in (0, 1)]
    rz_m = [pick((mz, cz), lambda r, o=o: r // 2 + o * half, lambda c: c) for o in (0, 1)]
    py_m = [pick((my, cy), lambda r: r // 2, lambda c, o=o: 2 * c + o) for o in (0, 1)]
    pz_m = [pick((cz, mz), lambda r: r, lambda c, o=o: c // 2 + o * half) for o in (0, 1)]

    def sum_fine(x):
        return dot(dot(ry_f, x), rz_f)

    def spread_fine(x):
        return dot(dot(py_f, x), pz_f)

    def sum_mid(x):
        return dot(dot(ry_m[0], x), rz_m[0]) + dot(dot(ry_m[1], x), rz_m[1])

    def spread_mid(x):
        return dot(py_m[0], dot(x, pz_m[0])) + dot(py_m[1], dot(x, pz_m[1]))

    def chunks(body):
        def step(i, _):
            body(pl.multiple_of(i * CHUNK, CHUNK))
            return 0
        lax.fori_loop(0, ny // CHUNK, step, 0)

    def prepare(p):
        def body(r):
            screen = RATE * counts_ref[p, pl.ds(r, CHUNK), :].astype(jnp.float32)
            d = 6.0 + screen
            c = DAMPING / d
            d_ref[p, pl.ds(r, CHUNK), :] = d
            c_ref[p, pl.ds(r, CHUNK), :] = c
            va[p, pl.ds(r + PAD, CHUNK), :] = c * f_ref[p, pl.ds(r, CHUNK), :]
        chunks(body)

    state = {"slot": 0}

    def exchange(v):
        k = state["slot"]
        state["slot"] += 1
        up = Transfer(v.at[3, rows, :], halo.at[k, 0], 1)
        down = Transfer(v.at[0, rows, :], halo.at[k, 1], -1)
        return k, up, down

    def neighbours(v, p, r, low, high):
        win = v[p, pl.ds(r, CHUNK + 2 * PAD), :]
        x = win[PAD:PAD + CHUNK]
        nb = win[PAD - 1:PAD - 1 + CHUNK] + win[PAD + 1:PAD + 1 + CHUNK] + z_sides(x)
        nb += v[p - 1, pl.ds(r + PAD, CHUNK), :] if p > 0 else low
        nb += v[p + 1, pl.ds(r + PAD, CHUNK), :] if p < 3 else high
        return x, nb

    def relax(dst, v, k, planes):
        def body(r):
            for p in planes:
                x, nb = neighbours(v, p, r, halo[k, 0, pl.ds(r, CHUNK), :], halo[k, 1, pl.ds(r, CHUNK), :])
                dst[p, pl.ds(r + PAD, CHUNK), :] = KEEP * x + c_ref[p, pl.ds(r, CHUNK), :] * (
                    f_ref[p, pl.ds(r, CHUNK), :] + nb)
        chunks(body)

    def relax_exchanged(dst, v, k, up, down):
        relax(dst, v, k, (1, 2))
        up.wait()
        down.wait()
        relax(dst, v, k, (0, 3))

    for p in (0, 3):
        prepare(p)
    pl.semaphore_wait(barrier, n - 1)
    first = exchange(va)
    first[1].start()
    first[2].start()
    for p in (1, 2):
        prepare(p)

    mid_screen = []
    for m in range(2):
        s = d_ref[2 * m] + d_ref[2 * m + 1] - 12.0
        mid_screen.append(0.125 * sum_fine(s))
        cm[2 + m] = DAMPING / (1.5 + mid_screen[m])
    cm_up = Transfer(cm.at[pl.ds(2, 2)], cm.at[pl.ds(0, 2)], 1).start()
    cm_down = Transfer(cm.at[pl.ds(2, 2)], cm.at[pl.ds(4, 2)], -1).start()
    gc[me] = DAMPING / (0.375 + 0.125 * sum_mid(mid_screen[0] + mid_screen[1]))
    gather_start(CYCLES, gc)

    lane = lax.broadcasted_iota(jnp.int32, (cy, cz), 1)
    row = lax.broadcasted_iota(jnp.int32, (cy, cz), 0)
    even = lane < half
    z_first, z_last = lax.rem(lane, half) == 0, lax.rem(lane, half) == half - 1

    def coarse_sides(x):
        w = pltpu.roll(x, half, 1)
        before = jnp.where(row == 0, 0.0, pltpu.roll(w, 1, 0))
        after = jnp.where(row == cy - 1, 0.0, pltpu.roll(w, cy - 1, 0))
        nb = w + jnp.where(even, before, after)
        nb += jnp.where(z_first, 0.0, pltpu.roll(x, 1, 1))
        return nb + jnp.where(z_last, 0.0, pltpu.roll(x, cz - 1, 1))

    GROUP = 4

    def coarse_sweep(dst, src):
        def body(g, _):
            for j in range(GROUP):
                q = g * GROUP + j
                x = src[q + 2]
                nb = coarse_sides(x) + src[q + 1] + src[q + 3]
                dst[q + 2] = KEEP * x + gr[CYCLES, q] + gc[q] * (0.0625 * nb)
            return 0
        lax.fori_loop(0, n // GROUP, body, 0)

    def vcycle(cycle, begun, spare, field):
        k, up, down = begun
        relax_exchanged(spare, field, k, up, down)
        quarters = []
        for side, p, dist in ((0, 3, 1), (1, 0, -1)):
            qown[cycle, side] = 0.5 * 0.25 * sum_fine(spare[p, rows, :])
            quarters.append(Transfer(qown.at[cycle, side], quarter.at[cycle, side], dist).start())
        kept, up, down = exchange(spare)
        up.start()
        down.start()

        for m in range(2):
            def body(r, m=m):
                total = None
                for p in (2 * m, 2 * m + 1):
                    x, nb = neighbours(spare, p, r, 0.0, 0.0)
                    res = f_ref[p, pl.ds(r, CHUNK), :] - d_ref[p, pl.ds(r, CHUNK), :] * x + nb
                    total = res if total is None else total + res
                rs[m, pl.ds(r, CHUNK), :] = total
            chunks(body)
        for m in range(2):
            rm[cycle, 2 + m] = 0.125 * sum_fine(rs[m])
        for t in quarters:
            t.wait()
        rm[cycle, 2] += quarter[cycle, 0]
        rm[cycle, 3] += quarter[cycle, 1]
        rm_up = Transfer(rm.at[cycle, pl.ds(2, 2)], rm.at[cycle, pl.ds(0, 2)], 1).start()
        rm_down = Transfer(rm.at[cycle, pl.ds(2, 2)], rm.at[cycle, pl.ds(4, 2)], -1).start()
        if cycle == 0:
            cm_up.wait()
            cm_down.wait()
        rm_up.wait()
        rm_down.wait()
        for q in range(6):
            ea[q + 1] = cm[q] * rm[cycle, q]

        def mid_relax(dst, src, m):
            x = src[m + 3]
            nb = y_sides(x) + z_sides(x) + src[m + 2] + src[m + 4]
            dst[m + 3] = KEEP * x + cm[m + 2] * (rm[cycle, m + 2] + 0.25 * nb)

        for m in range(-1, 3):
            mid_relax(e2.at[cycle], ea, m)
        wide = [Transfer(e2.at[cycle, a], e2.at[cycle, b], dist).start()
                for a, b, dist in ((3, 1, 1), (4, 6, -1), (4, 0, 2), (3, 7, -2))]
        total = 0.0
        for m in range(2):
            x = e2[cycle, m + 3]
            nb = y_sides(x) + z_sides(x) + e2[cycle, m + 2] + e2[cycle, m + 4]
            total += rm[cycle, m + 2] - DAMPING / cm[m + 2] * x + 0.25 * nb
        gr[cycle, me] = 0.125 * sum_mid(total)
        gather_start(cycle, gr.at[cycle])
        if cycle == 0:
            gather_wait(CYCLES, gc)
        gather_wait(cycle, gr.at[cycle])

        def begin(q, _):
            g = gc[q] * gr[cycle, q]
            gr[CYCLES, q] = g
            xa[q + 2] = g
            return 0

        lax.fori_loop(0, n, begin, 0)

        def twice(_, c):
            coarse_sweep(xb, xa)
            coarse_sweep(xa, xb)
            return c

        lax.fori_loop(0, (COARSE - 1) // 2, twice, 0)
        coarse_sweep(xb, xa)

        for t in wide:
            t.wait()
        for j in range(5):
            e = spread_mid(xb[me + j])
            for m in (2 * (j - 2), 2 * (j - 2) + 1):
                if -3 <= m <= 4:
                    ea[m + 3] = e2[cycle, m + 3] + e
        for m in range(-2, 4):
            mid_relax(eb, ea, m)
        for m in range(-1, 3):
            mid_relax(ea, eb, m)
        up.wait()
        down.wait()
        for m in range(-1, 3):
            e = spread_fine(ea[m + 3])
            if m == -1:
                @pl.when(me > 0)
                def _():
                    halo[kept, 0] += e
            elif m == 2:
                @pl.when(me < n - 1)
                def _():
                    halo[kept, 1] += e
            else:
                for p in (2 * m, 2 * m + 1):
                    spare[p, rows, :] += e
        for p_pair in ((0, 3), (1, 2)):
            relax(field, spare, kept, p_pair)
            if p_pair == (0, 3):
                post = exchange(field)
                post[1].start()
                post[2].start()
        relax_exchanged(spare, field, *post)
        return spare, field

    done, spare = vcycle(0, first, vb, va)
    again = exchange(done)
    again[1].start()
    again[2].start()
    relax_exchanged(spare, done, *again)
    begun = exchange(spare)
    begun[1].start()
    begun[2].start()
    done, spare = vcycle(1, begun, done, spare)
    k = state["slot"]
    last = Transfer(done.at[0, rows, :], halo.at[k, 1], -1).start()
    for p in range(4):
        out_ref[p] = done[p, rows, :]
    last.wait()
    ahead_ref[0] = halo[k, 1]


def shards(n, cotangent, counts):
    nx, ny, nz = cotangent.shape
    f32 = jnp.float32
    my, mz = ny // 2, nz // 2
    cy, cz = my // 4, mz
    vmem = pl.BlockSpec(memory_space=pltpu.VMEM)
    slots = 8
    multiplier, following = pl.pallas_call(
        functools.partial(kernel, n),
        out_shape=(jax.ShapeDtypeStruct((nx, ny, nz), f32), jax.ShapeDtypeStruct((1, ny, nz), f32)),
        in_specs=[vmem, vmem],
        out_specs=(vmem, vmem),
        scratch_shapes=[
            pltpu.VMEM((nx, ny + 2 * PAD, nz), f32),
            pltpu.VMEM((nx, ny + 2 * PAD, nz), f32),
            pltpu.VMEM((nx, ny, nz), f32),
            pltpu.VMEM((nx, ny, nz), f32),
            pltpu.VMEM((slots, 2, ny, nz), f32),
            pltpu.VMEM((CYCLES, 2, my, mz), f32),
            pltpu.VMEM((2, ny, nz), f32),
            pltpu.VMEM((6, my, mz), f32),
            pltpu.VMEM((CYCLES, 6, my, mz), f32),
            pltpu.VMEM((CYCLES, 8, my, mz), f32),
            pltpu.VMEM((8, my, mz), f32),
            pltpu.VMEM((8, my, mz), f32),
            pltpu.VMEM((CYCLES, 2, my, mz), f32),
            pltpu.VMEM((n, cy, cz), f32),
            pltpu.VMEM((CYCLES + 1, n, cy, cz), f32),
            pltpu.VMEM((n + 4, cy, cz), f32),
            pltpu.VMEM((n + 4, cy, cz), f32),
            pltpu.SemaphoreType.DMA((40,)),
            pltpu.SemaphoreType.DMA((40,)),
            pltpu.SemaphoreType.DMA((CYCLES + 1, n)),
            pltpu.SemaphoreType.DMA((CYCLES + 1, n)),
        ],
        compiler_params=pltpu.CompilerParams(
            collective_id=0, has_side_effects=True, vmem_limit_bytes=40 * 1024 * 1024),
    )(cotangent, counts)
    ahead_x = jnp.concatenate([multiplier[1:], following], axis=0)
    ahead_y = jnp.pad(multiplier[:, 1:], ((0, 0), (0, 1), (0, 0)))
    ahead_z = jnp.pad(multiplier[:, :, 1:], ((0, 0), (0, 0), (0, 1)))
    normal_grad = jnp.stack([multiplier - ahead_x, multiplier - ahead_y, multiplier - ahead_z])
    return (multiplier, normal_grad)


def solution(mesh):
    split = P(("scene", "gx"), None, None)
    return jax.shard_map(
        functools.partial(shards, mesh.shape["gx"]),
        mesh=mesh,
        in_specs=(split, split),
        out_specs=(split, P(None, ("scene", "gx"), None, None)),
        check_vma=False,
    )
```

```python
import functools

import jax
import jax.numpy as jnp
from jax import lax
from jax.experimental import pallas as pl
from jax.experimental.pallas import tpu as pltpu
from jax.sharding import PartitionSpec as P

SWEEPS = 2
COARSE = 16
CYCLES = 2
DAMPING = 0.8
KEEP = 1.0 - DAMPING
RATE = 0.004
MESH = pl.DeviceIdType.MESH
PAD = 8
CHUNK = 32


def dot(a, b):
    return lax.dot(a, b, preferred_element_type=jnp.float32)


def pick(shape, row_of, column_of):
    r = lax.broadcasted_iota(jnp.int32, shape, 0)
    c = lax.broadcasted_iota(jnp.int32, shape, 1)
    return jnp.where(row_of(r) == column_of(c), 1.0, 0.0).astype(jnp.bfloat16)


def z_sides(x):
    last = x.shape[1] - 1
    lane = lax.broadcasted_iota(jnp.int32, x.shape, 1)
    before = jnp.where(lane == 0, 0.0, pltpu.roll(x, 1, 1))
    return before + jnp.where(lane == last, 0.0, pltpu.roll(x, last, 1))


def y_sides(x):
    last = x.shape[0] - 1
    row = lax.broadcasted_iota(jnp.int32, x.shape, 0)
    before = jnp.where(row == 0, 0.0, pltpu.roll(x, 1, 0))
    return before + jnp.where(row == last, 0.0, pltpu.roll(x, last, 0))


def split(x):
    high = x.astype(jnp.bfloat16)
    return high, (x - high.astype(jnp.float32)).astype(jnp.bfloat16)


def times(x, matrix):
    high, low = split(x)
    return dot(high, matrix) + dot(low, matrix)


def timed(matrix, x):
    high, low = split(x)
    return dot(matrix, high) + dot(matrix, low)


def kernel(n, f_hbm, counts_hbm, out_ref, ahead_ref, f_ref, counts_ref, va, vb, vd, ve, c_ref, d_ref, last,
           quarter, rs, cm, rm, e2, ea, eb, qown, gc, gr, xa, xb, lsem, fsend, frecv, gsend, grecv):
    me = lax.axis_index("gx")
    ny, nz = f_hbm.shape[1:]
    my, mz = ny // 2, nz // 2
    cy, cz = my // 4, mz
    rows = pl.ds(PAD, ny)

    local = [pltpu.make_async_copy(f_hbm, f_ref.at[pl.ds(1, 4)], lsem.at[0]),
             pltpu.make_async_copy(counts_hbm, counts_ref.at[pl.ds(1, 4)], lsem.at[1])]
    for copy in local:
        copy.start()

    for ref in (va, vb, vd, ve):
        for p in range(ref.shape[0]):
            ref[p, pl.ds(0, PAD), :] = jnp.zeros((PAD, nz), jnp.float32)
            ref[p, pl.ds(PAD + ny, PAD), :] = jnp.zeros((PAD, nz), jnp.float32)
    cm[...] = jnp.zeros_like(cm)
    rm[...] = jnp.zeros_like(rm)
    e2[...] = jnp.zeros_like(e2)
    quarter[...] = jnp.zeros_like(quarter)
    for ref in (xa, xb):
        for p in (0, 1, n + 2, n + 3):
            ref[p] = jnp.zeros((cy, cz), jnp.float32)

    def clear(side):
        for ref in (vb, vd, ve):
            for p in (6 * side, 6 * side + 1):
                ref[p, rows, :] = jnp.zeros((ny, nz), jnp.float32)
        f_ref[5 * side] = jnp.zeros((ny, nz), jnp.float32)
        counts_ref[5 * side] = jnp.zeros((ny, nz), jnp.int32)

    @pl.when(me == 0)
    def _():
        clear(0)

    @pl.when(me == n - 1)
    def _():
        clear(1)
        last[...] = jnp.zeros_like(last)

    barrier = pltpu.get_barrier_semaphore()

    def greet(k, _):
        pl.semaphore_signal(barrier, inc=1, device_id={"gx": lax.rem(me + k, n)}, device_id_type=MESH)
        return 0

    lax.fori_loop(1, n, greet, 0)

    used = [0]

    class Transfer:
        def __init__(self, src, dst, dist):
            self.dist, self.src, self.dst, self.j = dist, src, dst, used[0]
            used[0] += 1

        def copy(self):
            return pltpu.make_async_remote_copy(
                src_ref=self.src, dst_ref=self.dst, send_sem=fsend.at[self.j],
                recv_sem=frecv.at[self.j], device_id={"gx": me + self.dist}, device_id_type=MESH)

        def inside(self, sign):
            return me < n - self.dist * sign if self.dist * sign > 0 else me >= -self.dist * sign

        def start(self):
            @pl.when(self.inside(1))
            def _():
                self.copy().start()
            return self

        def arrived(self):
            @pl.when(self.inside(-1))
            def _():
                self.copy().wait_recv()

        def sent(self):
            @pl.when(self.inside(1))
            def _():
                self.copy().wait_send()

        def wait(self):
            self.arrived()
            self.sent()

    def gather_copy(g, ref, k, peer, owner):
        return pltpu.make_async_remote_copy(
            src_ref=ref.at[owner], dst_ref=ref.at[owner], send_sem=gsend.at[g, k],
            recv_sem=grecv.at[g, k], device_id={"gx": peer}, device_id_type=MESH)

    def gather_start(g, ref):
        def body(k, _):
            gather_copy(g, ref, k, lax.rem(me + k, n), me).start()
            return 0
        lax.fori_loop(1, n, body, 0)

    def gather_wait(g, ref):
        def body(k, _):
            c = gather_copy(g, ref, k, lax.rem(me + k, n), lax.rem(me + n - k, n))
            c.wait_recv()
            c.wait_send()
            return 0
        lax.fori_loop(1, n, body, 0)

    ry_f = pick((my, ny), lambda r: r, lambda c: c // 2)
    rz_f = pick((nz, mz), lambda r: r // 2, lambda c: c)
    py_f = pick((ny, my), lambda r: r // 2, lambda c: c)
    pz_f = pick((mz, nz), lambda r: r, lambda c: c // 2)
    half = mz // 2
    ry_m = [pick((cy, my), lambda r, o=o: 2 * r + o, lambda c: c // 2) for o in (0, 1)]
    rz_m = [pick((mz, cz), lambda r, o=o: r // 2 + o * half, lambda c: c) for o in (0, 1)]
    py_m = [pick((my, cy), lambda r: r // 2, lambda c, o=o: 2 * c + o) for o in (0, 1)]
    pz_m = [pick((cz, mz), lambda r: r, lambda c, o=o: c // 2 + o * half) for o in (0, 1)]

    def sum_fine(x):
        return times(timed(ry_f, x), rz_f)

    def spread_fine(x):
        return times(timed(py_f, x), pz_f)

    def sum_mid(x):
        return times(timed(ry_m[0], x), rz_m[0]) + times(timed(ry_m[1], x), rz_m[1])

    def spread_mid(x):
        return timed(py_m[0], times(x, pz_m[0])) + timed(py_m[1], times(x, pz_m[1]))

    def chunks(body):
        def step(i, _):
            body(pl.multiple_of(i * CHUNK, CHUNK))
            return 0
        lax.fori_loop(0, ny // CHUNK, step, 0)

    below, above = jnp.where(me > 0, DAMPING, 0.0), jnp.where(me < n - 1, DAMPING, 0.0)

    def prepare(planes):
        def body(r):
            at = pl.ds(r, CHUNK)
            for p in planes:
                d = 6.0 + RATE * counts_ref[p + 1, at, :].astype(jnp.float32)
                c = (below if p < 0 else above if p > 3 else DAMPING) / d
                if 0 <= p < 4:
                    d_ref[p, at, :] = d
                c_ref[p + 1, at, :] = c
                va[p + 2, pl.ds(r + PAD, CHUNK), :] = c * f_ref[p + 1, at, :]
        chunks(body)

    def neighbours(v, p, r, low=None, high=None):
        at = pl.ds(r + PAD, CHUNK)
        win = v[p + 2, pl.ds(r, CHUNK + 2 * PAD), :]
        x = win[PAD:PAD + CHUNK]
        nb = win[PAD - 1:PAD - 1 + CHUNK] + win[PAD + 1:PAD + 1 + CHUNK] + z_sides(x)
        for q, given in ((p - 1, low), (p + 1, high)):
            if given is None:
                nb += v[q + 2, at, :]
            elif given is not False:
                nb += given[0, pl.ds(r, CHUNK), :]
        return x, nb

    def relax(dst, v, planes, high=None, raw=False):
        def body(r):
            at = pl.ds(r, CHUNK)
            for p in planes:
                x, nb = neighbours(v, p, r, None, high)
                new = KEEP * x + c_ref[p + 1, at, :] * (f_ref[p + 1, at, :] + nb)
                if raw:
                    dst[p, at, :] = new
                else:
                    dst[p + 2, pl.ds(r + PAD, CHUNK), :] = new
        chunks(body)

    def share(v):
        return [Transfer(v.at[pl.ds(4, 2), rows, :], v.at[pl.ds(0, 2), rows, :], 1).start(),
                Transfer(v.at[pl.ds(2, 2), rows, :], v.at[pl.ds(6, 2), rows, :], -1).start()]

    pl.semaphore_wait(barrier, n - 1)
    first = []
    for src, ref in ((counts_hbm, counts_ref), (f_hbm, f_ref)):
        first.append(Transfer(src.at[3], ref.at[0], 1).start())
        first.append(Transfer(src.at[0], ref.at[5], -1).start())
    for copy in local:
        copy.wait()
    prepare((0, 1, 2, 3))

    mid_screen = []
    for m in range(2):
        s = d_ref[2 * m] + d_ref[2 * m + 1] - 12.0
        mid_screen.append(0.125 * sum_fine(s))
        cm[2 + m] = DAMPING / (1.5 + mid_screen[m])
    cm_up = Transfer(cm.at[pl.ds(2, 2)], cm.at[pl.ds(0, 2)], 1).start()
    cm_down = Transfer(cm.at[pl.ds(2, 2)], cm.at[pl.ds(4, 2)], -1).start()
    gc[me] = DAMPING / (0.375 + 0.125 * sum_mid(mid_screen[0] + mid_screen[1]))
    gather_start(CYCLES, gc)

    lane = lax.broadcasted_iota(jnp.int32, (cy, cz), 1)
    row = lax.broadcasted_iota(jnp.int32, (cy, cz), 0)
    even = lane < half
    z_first, z_last = lax.rem(lane, half) == 0, lax.rem(lane, half) == half - 1

    def coarse_sides(x):
        w = pltpu.roll(x, half, 1)
        before = jnp.where(row == 0, 0.0, pltpu.roll(w, 1, 0))
        after = jnp.where(row == cy - 1, 0.0, pltpu.roll(w, cy - 1, 0))
        nb = w + jnp.where(even, before, after)
        nb += jnp.where(z_first, 0.0, pltpu.roll(x, 1, 1))
        return nb + jnp.where(z_last, 0.0, pltpu.roll(x, cz - 1, 1))

    GROUP = 16 if n % 16 == 0 else 4

    def coarse_sweep(dst, src):
        def body(g, _):
            for j in range(GROUP):
                q = g * GROUP + j
                x = src[q + 2]
                nb = coarse_sides(x) + src[q + 1] + src[q + 3]
                dst[q + 2] = KEEP * x + gr[CYCLES, q] + gc[q] * (0.0625 * nb)
            return 0
        lax.fori_loop(0, n // GROUP, body, 0)

    def vcycle(cycle, v):
        swaps = []
        for side, p, dist in ((0, 3, 1), (1, 0, -1)):
            qown[cycle, side] = 0.5 * 0.25 * sum_fine(v[p + 2, rows, :])
            for far in (1, 2):
                swaps.append(Transfer(qown.at[cycle, side], quarter.at[cycle, far - 1, side], far * dist).start())
        for m in range(2):
            def body(r, m=m):
                total = None
                for p in (2 * m, 2 * m + 1):
                    x, nb = neighbours(v, p, r, False if p == 0 else None, False if p == 3 else None)
                    res = f_ref[p + 1, pl.ds(r, CHUNK), :] - d_ref[p, pl.ds(r, CHUNK), :] * x + nb
                    total = res if total is None else total + res
                rs[m, pl.ds(r, CHUNK), :] = total
            chunks(body)
        for m in range(2):
            rm[cycle, 2 + m] = 0.125 * sum_fine(rs[m])
        swaps.append(Transfer(rm.at[cycle, pl.ds(2, 2)], rm.at[cycle, pl.ds(0, 2)], 1).start())
        swaps.append(Transfer(rm.at[cycle, pl.ds(2, 2)], rm.at[cycle, pl.ds(4, 2)], -1).start())
        if cycle == 0:
            cm_up.wait()
            cm_down.wait()
        for s in swaps:
            s.wait()
        rm[cycle, 0] += quarter[cycle, 1, 0]
        rm[cycle, 1] += qown[cycle, 1]
        rm[cycle, 2] += quarter[cycle, 0, 0]
        rm[cycle, 3] += quarter[cycle, 0, 1]
        rm[cycle, 4] += qown[cycle, 0]
        rm[cycle, 5] += quarter[cycle, 1, 1]
        for q in range(6):
            ea[q + 1] = cm[q] * rm[cycle, q]

        def mid_relax(dst, src, m):
            x = src[m + 3]
            nb = y_sides(x) + z_sides(x) + src[m + 2] + src[m + 4]
            dst[m + 3] = KEEP * x + cm[m + 2] * (rm[cycle, m + 2] + 0.25 * nb)

        for m in range(-1, 3):
            mid_relax(e2.at[cycle], ea, m)
        wide = [Transfer(e2.at[cycle, a], e2.at[cycle, b], dist).start()
                for a, b, dist in ((3, 1, 1), (4, 6, -1), (4, 0, 2), (3, 7, -2))]
        total = 0.0
        for m in range(2):
            x = e2[cycle, m + 3]
            nb = y_sides(x) + z_sides(x) + e2[cycle, m + 2] + e2[cycle, m + 4]
            total += rm[cycle, m + 2] - DAMPING / cm[m + 2] * x + 0.25 * nb
        gr[cycle, me] = 0.125 * sum_mid(total)
        gather_start(cycle, gr.at[cycle])
        wide += share(v)
        if cycle == 0:
            gather_wait(CYCLES, gc)
        gather_wait(cycle, gr.at[cycle])

        def begin(q, _):
            g = gc[q] * gr[cycle, q]
            gr[CYCLES, q] = g
            xa[q + 2] = g
            return 0

        lax.fori_loop(0, n, begin, 0)

        def twice(_, c):
            coarse_sweep(xb, xa)
            coarse_sweep(xa, xb)
            return c

        lax.fori_loop(0, (COARSE - 1) // 2, twice, 0)
        coarse_sweep(xb, xa)

        for t in wide:
            t.wait()
        for j in range(5):
            e = spread_mid(xb[me + j])
            for m in (2 * (j - 2), 2 * (j - 2) + 1):
                if -3 <= m <= 4:
                    ea[m + 3] = e2[cycle, m + 3] + e
        for m in range(-2, 4):
            mid_relax(eb, ea, m)
        for m in range(-1, 3):
            mid_relax(ea, eb, m)
        for m in range(-1, 3):
            e = spread_fine(ea[m + 3])
            for p in (2 * m, 2 * m + 1):
                v[p + 2, rows, :] += e

    for t in first:
        t.wait()
    prepare((-1, 4))
    relax(vb, va, (0, 3))
    relax(vb, va, (1, 2))
    vcycle(0, vb)
    relax(va, vb, (-1, 0, 1))
    relax(va, vb, (2, 3, 4))
    relax(vd, va, (0, 1))
    relax(vd, va, (2, 3))
    shared = share(vd)
    relax(va, vd, (1, 2))
    for t in shared:
        t.wait()
    relax(va, vd, (0, 3))
    relax(va, vd, (-1, 4))
    relax(ve, va, (0, 3))
    relax(ve, va, (1, 2))
    vcycle(1, ve)
    relax(va, ve, (0, 1))
    beyond = Transfer(va.at[pl.ds(3, 1), rows, :], last, -1).start()
    relax(va, ve, (-1, 2))
    relax(va, ve, (3, 4))
    relax(out_ref, va, (0, 1), raw=True)
    relax(out_ref, va, (2, 3), raw=True)
    beyond.wait()

    def body(r):
        at = pl.ds(r, CHUNK)
        x, nb = neighbours(va, 4, r, None, last)
        ahead_ref[0, at, :] = KEEP * x + c_ref[5, at, :] * (f_ref[5, at, :] + nb)

    chunks(body)


def shards(n, cotangent, counts):
    nx, ny, nz = cotangent.shape
    f32 = jnp.float32
    my, mz = ny // 2, nz // 2
    cy, cz = my // 4, mz
    vmem = pl.BlockSpec(memory_space=pltpu.VMEM)
    anywhere = pl.BlockSpec(memory_space=pl.ANY)
    multiplier, following = pl.pallas_call(
        functools.partial(kernel, n),
        out_shape=(jax.ShapeDtypeStruct((nx, ny, nz), f32), jax.ShapeDtypeStruct((1, ny, nz), f32)),
        in_specs=[anywhere, anywhere],
        out_specs=(vmem, vmem),
        scratch_shapes=[
            pltpu.VMEM((nx + 2, ny, nz), f32),
            pltpu.VMEM((nx + 2, ny, nz), jnp.int32),
            pltpu.VMEM((nx + 4, ny + 2 * PAD, nz), f32),
            pltpu.VMEM((nx + 4, ny + 2 * PAD, nz), f32),
            pltpu.VMEM((nx + 4, ny + 2 * PAD, nz), f32),
            pltpu.VMEM((nx + 4, ny + 2 * PAD, nz), f32),
            pltpu.VMEM((nx + 2, ny, nz), f32),
            pltpu.VMEM((nx, ny, nz), f32),
            pltpu.VMEM((1, ny, nz), f32),
            pltpu.VMEM((CYCLES, 2, 2, my, mz), f32),
            pltpu.VMEM((2, ny, nz), f32),
            pltpu.VMEM((6, my, mz), f32),
            pltpu.VMEM((CYCLES, 6, my, mz), f32),
            pltpu.VMEM((CYCLES, 8, my, mz), f32),
            pltpu.VMEM((8, my, mz), f32),
            pltpu.VMEM((8, my, mz), f32),
            pltpu.VMEM((CYCLES, 2, my, mz), f32),
            pltpu.VMEM((n, cy, cz), f32),
            pltpu.VMEM((CYCLES + 1, n, cy, cz), f32),
            pltpu.VMEM((n + 4, cy, cz), f32),
            pltpu.VMEM((n + 4, cy, cz), f32),
            pltpu.SemaphoreType.DMA((2,)),
            pltpu.SemaphoreType.DMA((40,)),
            pltpu.SemaphoreType.DMA((40,)),
            pltpu.SemaphoreType.DMA((CYCLES + 1, n)),
            pltpu.SemaphoreType.DMA((CYCLES + 1, n)),
        ],
        compiler_params=pltpu.CompilerParams(
            collective_id=0, has_side_effects=True, vmem_limit_bytes=40 * 1024 * 1024),
    )(cotangent, counts)
    ahead_x = jnp.concatenate([multiplier[1:], following], axis=0)
    ahead_y = jnp.pad(multiplier[:, 1:], ((0, 0), (0, 1), (0, 0)))
    ahead_z = jnp.pad(multiplier[:, :, 1:], ((0, 0), (0, 0), (0, 1)))
    normal_grad = jnp.stack([multiplier - ahead_x, multiplier - ahead_y, multiplier - ahead_z])
    return (multiplier, normal_grad)


def solution(mesh):
    split = P(("scene", "gx"), None, None)
    return jax.shard_map(
        functools.partial(shards, mesh.shape["gx"]),
        mesh=mesh,
        in_specs=(split, split),
        out_specs=(split, P(None, ("scene", "gx"), None, None)),
        check_vma=False,
    )
```

```python
import functools

import jax
import jax.numpy as jnp
from jax import lax
from jax.experimental import pallas as pl
from jax.experimental.pallas import tpu as pltpu
from jax.sharding import PartitionSpec as P

SWEEPS = 2
COARSE = 16
CYCLES = 2
DAMPING = 0.8
KEEP = 1.0 - DAMPING
RATE = 0.004
MESH = pl.DeviceIdType.MESH
PAD = 8
CHUNK = 128


def dot(a, b):
    return lax.dot(a, b, preferred_element_type=jnp.float32)


def pick(shape, row_of, column_of):
    r = lax.broadcasted_iota(jnp.int32, shape, 0)
    c = lax.broadcasted_iota(jnp.int32, shape, 1)
    return jnp.where(row_of(r) == column_of(c), 1.0, 0.0).astype(jnp.bfloat16)


def z_sides(x):
    last = x.shape[1] - 1
    lane = lax.broadcasted_iota(jnp.int32, x.shape, 1)
    before = jnp.where(lane == 0, 0.0, pltpu.roll(x, 1, 1))
    return before + jnp.where(lane == last, 0.0, pltpu.roll(x, last, 1))


def y_sides(x):
    last = x.shape[0] - 1
    row = lax.broadcasted_iota(jnp.int32, x.shape, 0)
    before = jnp.where(row == 0, 0.0, pltpu.roll(x, 1, 0))
    return before + jnp.where(row == last, 0.0, pltpu.roll(x, last, 0))


def split(x):
    high = x.astype(jnp.bfloat16)
    return high, (x - high.astype(jnp.float32)).astype(jnp.bfloat16)


def times(x, matrix):
    high, low = split(x)
    return dot(high, matrix) + dot(low, matrix)


def timed(matrix, x):
    high, low = split(x)
    return dot(matrix, high) + dot(matrix, low)


def kernel(n, f_hbm, counts_hbm, out_ref, ahead_ref, f_ref, counts_ref, va, vb, vd, ve, c_ref, d_ref, last,
           quarter, rs, cm, rm, e2, ea, eb, qown, gc, gr, xa, xb, lsem, fsend, frecv, gsend, grecv):
    me = lax.axis_index("gx")
    ny, nz = f_hbm.shape[1:]
    my, mz = ny // 2, nz // 2
    cy, cz = my // 4, mz
    rows = pl.ds(PAD, ny)

    local = [pltpu.make_async_copy(f_hbm, f_ref.at[pl.ds(1, 4)], lsem.at[0]),
             pltpu.make_async_copy(counts_hbm, counts_ref.at[pl.ds(1, 4)], lsem.at[1])]
    for copy in local:
        copy.start()

    for ref in (va, vb, vd, ve):
        for p in range(ref.shape[0]):
            ref[p, pl.ds(0, PAD), :] = jnp.zeros((PAD, nz), jnp.float32)
            ref[p, pl.ds(PAD + ny, PAD), :] = jnp.zeros((PAD, nz), jnp.float32)
    cm[...] = jnp.zeros_like(cm)
    rm[...] = jnp.zeros_like(rm)
    e2[...] = jnp.zeros_like(e2)
    quarter[...] = jnp.zeros_like(quarter)
    for ref in (xa, xb):
        for p in (0, 1, n + 2, n + 3):
            ref[p] = jnp.zeros((cy, cz), jnp.float32)

    def clear(side):
        for ref in (vb, vd, ve):
            for p in (6 * side, 6 * side + 1):
                ref[p, rows, :] = jnp.zeros((ny, nz), jnp.float32)
        f_ref[5 * side] = jnp.zeros((ny, nz), jnp.float32)
        counts_ref[5 * side] = jnp.zeros((ny, nz), jnp.int32)

    @pl.when(me == 0)
    def _():
        clear(0)

    @pl.when(me == n - 1)
    def _():
        clear(1)
        last[...] = jnp.zeros_like(last)

    barrier = pltpu.get_barrier_semaphore()

    def greet(k, _):
        pl.semaphore_signal(barrier, inc=1, device_id={"gx": lax.rem(me + k, n)}, device_id_type=MESH)
        return 0

    lax.fori_loop(1, n, greet, 0)

    used = [0]

    class Transfer:
        def __init__(self, src, dst, dist):
            self.dist, self.src, self.dst, self.j = dist, src, dst, used[0]
            used[0] += 1

        def copy(self):
            return pltpu.make_async_remote_copy(
                src_ref=self.src, dst_ref=self.dst, send_sem=fsend.at[self.j],
                recv_sem=frecv.at[self.j], device_id={"gx": me + self.dist}, device_id_type=MESH)

        def inside(self, sign):
            return me < n - self.dist * sign if self.dist * sign > 0 else me >= -self.dist * sign

        def start(self):
            @pl.when(self.inside(1))
            def _():
                self.copy().start()
            return self

        def arrived(self):
            @pl.when(self.inside(-1))
            def _():
                self.copy().wait_recv()

        def sent(self):
            @pl.when(self.inside(1))
            def _():
                self.copy().wait_send()

        def wait(self):
            self.arrived()
            self.sent()

    def gather_copy(g, ref, k, peer, owner):
        return pltpu.make_async_remote_copy(
            src_ref=ref.at[owner], dst_ref=ref.at[owner], send_sem=gsend.at[g, k],
            recv_sem=grecv.at[g, k], device_id={"gx": peer}, device_id_type=MESH)

    def gather_start(g, ref):
        def body(k, _):
            gather_copy(g, ref, k, lax.rem(me + k, n), me).start()
            return 0
        lax.fori_loop(1, n, body, 0)

    def gather_wait(g, ref):
        def body(k, _):
            c = gather_copy(g, ref, k, lax.rem(me + k, n), lax.rem(me + n - k, n))
            c.wait_recv()
            c.wait_send()
            return 0
        lax.fori_loop(1, n, body, 0)

    ry_f = pick((my, ny), lambda r: r, lambda c: c // 2)
    rz_f = pick((nz, mz), lambda r: r // 2, lambda c: c)
    py_f = pick((ny, my), lambda r: r // 2, lambda c: c)
    pz_f = pick((mz, nz), lambda r: r, lambda c: c // 2)
    half = mz // 2
    ry_m = [pick((cy, my), lambda r, o=o: 2 * r + o, lambda c: c // 2) for o in (0, 1)]
    rz_m = [pick((mz, cz), lambda r, o=o: r // 2 + o * half, lambda c: c) for o in (0, 1)]
    py_m = [pick((my, cy), lambda r: r // 2, lambda c, o=o: 2 * c + o) for o in (0, 1)]
    pz_m = [pick((cz, mz), lambda r: r, lambda c, o=o: c // 2 + o * half) for o in (0, 1)]

    def sum_fine(x):
        return times(timed(ry_f, x), rz_f)

    def spread_fine(x):
        return times(timed(py_f, x), pz_f)

    def sum_mid(x):
        return times(timed(ry_m[0], x), rz_m[0]) + times(timed(ry_m[1], x), rz_m[1])

    def spread_mid(x):
        return timed(py_m[0], times(x, pz_m[0])) + timed(py_m[1], times(x, pz_m[1]))

    def chunks(body):
        def step(i, _):
            body(pl.multiple_of(i * CHUNK, CHUNK))
            return 0
        lax.fori_loop(0, ny // CHUNK, step, 0)

    below, above = jnp.where(me > 0, DAMPING, 0.0), jnp.where(me < n - 1, DAMPING, 0.0)

    def prepare(planes):
        def body(r):
            at = pl.ds(r, CHUNK)
            for p in planes:
                d = 6.0 + RATE * counts_ref[p + 1, at, :].astype(jnp.float32)
                c = (below if p < 0 else above if p > 3 else DAMPING) / d
                if 0 <= p < 4:
                    d_ref[p, at, :] = d
                c_ref[p + 1, at, :] = c
                va[p + 2, pl.ds(r + PAD, CHUNK), :] = c * f_ref[p + 1, at, :]
        chunks(body)

    def neighbours(v, p, r, low=None, high=None):
        at = pl.ds(r + PAD, CHUNK)
        win = v[p + 2, pl.ds(r, CHUNK + 2 * PAD), :]
        x = win[PAD:PAD + CHUNK]
        nb = win[PAD - 1:PAD - 1 + CHUNK] + win[PAD + 1:PAD + 1 + CHUNK] + z_sides(x)
        for q, given in ((p - 1, low), (p + 1, high)):
            if given is None:
                nb += v[q + 2, at, :]
            elif given is not False:
                nb += given[0, pl.ds(r, CHUNK), :]
        return x, nb

    def relax(dst, v, planes, high=None, raw=False):
        def body(r):
            at = pl.ds(r, CHUNK)
            for p in planes:
                x, nb = neighbours(v, p, r, None, high)
                new = KEEP * x + c_ref[p + 1, at, :] * (f_ref[p + 1, at, :] + nb)
                if raw:
                    dst[p, at, :] = new
                else:
                    dst[p + 2, pl.ds(r + PAD, CHUNK), :] = new
        chunks(body)

    def share(v):
        return [Transfer(v.at[pl.ds(4, 2), rows, :], v.at[pl.ds(0, 2), rows, :], 1).start(),
                Transfer(v.at[pl.ds(2, 2), rows, :], v.at[pl.ds(6, 2), rows, :], -1).start()]

    pl.semaphore_wait(barrier, n - 1)
    first = []
    for src, ref in ((counts_hbm, counts_ref), (f_hbm, f_ref)):
        first.append(Transfer(src.at[3], ref.at[0], 1).start())
        first.append(Transfer(src.at[0], ref.at[5], -1).start())
    for copy in local:
        copy.wait()
    prepare((0, 1, 2, 3))

    mid_screen = []
    for m in range(2):
        s = d_ref[2 * m] + d_ref[2 * m + 1] - 12.0
        mid_screen.append(0.125 * sum_fine(s))
        cm[2 + m] = DAMPING / (1.5 + mid_screen[m])
    cm_up = Transfer(cm.at[pl.ds(2, 2)], cm.at[pl.ds(0, 2)], 1).start()
    cm_down = Transfer(cm.at[pl.ds(2, 2)], cm.at[pl.ds(4, 2)], -1).start()
    gc[me] = DAMPING / (0.375 + 0.125 * sum_mid(mid_screen[0] + mid_screen[1]))
    gather_start(CYCLES, gc)

    lane = lax.broadcasted_iota(jnp.int32, (cy, cz), 1)
    row = lax.broadcasted_iota(jnp.int32, (cy, cz), 0)
    even = lane < half
    z_first, z_last = lax.rem(lane, half) == 0, lax.rem(lane, half) == half - 1

    def coarse_sides(x):
        w = pltpu.roll(x, half, 1)
        before = jnp.where(row == 0, 0.0, pltpu.roll(w, 1, 0))
        after = jnp.where(row == cy - 1, 0.0, pltpu.roll(w, cy - 1, 0))
        nb = w + jnp.where(even, before, after)
        nb += jnp.where(z_first, 0.0, pltpu.roll(x, 1, 1))
        return nb + jnp.where(z_last, 0.0, pltpu.roll(x, cz - 1, 1))

    GROUP = 16 if n % 16 == 0 else 4

    def coarse_sweep(dst, src):
        def body(g, _):
            for j in range(GROUP):
                q = g * GROUP + j
                x = src[q + 2]
                nb = coarse_sides(x) + src[q + 1] + src[q + 3]
                dst[q + 2] = KEEP * x + gr[CYCLES, q] + gc[q] * (0.0625 * nb)
            return 0
        lax.fori_loop(0, n // GROUP, body, 0)

    def vcycle(cycle, v):
        swaps = []
        for side, p, dist in ((0, 3, 1), (1, 0, -1)):
            qown[cycle, side] = 0.5 * 0.25 * sum_fine(v[p + 2, rows, :])
            for far in (1, 2):
                swaps.append(Transfer(qown.at[cycle, side], quarter.at[cycle, far - 1, side], far * dist).start())
        for m in range(2):
            def body(r, m=m):
                total = None
                for p in (2 * m, 2 * m + 1):
                    x, nb = neighbours(v, p, r, False if p == 0 else None, False if p == 3 else None)
                    res = f_ref[p + 1, pl.ds(r, CHUNK), :] - d_ref[p, pl.ds(r, CHUNK), :] * x + nb
                    total = res if total is None else total + res
                rs[m, pl.ds(r, CHUNK), :] = total
            chunks(body)
        for m in range(2):
            rm[cycle, 2 + m] = 0.125 * sum_fine(rs[m])
        swaps.append(Transfer(rm.at[cycle, pl.ds(2, 2)], rm.at[cycle, pl.ds(0, 2)], 1).start())
        swaps.append(Transfer(rm.at[cycle, pl.ds(2, 2)], rm.at[cycle, pl.ds(4, 2)], -1).start())
        if cycle == 0:
            cm_up.wait()
            cm_down.wait()
        for s in swaps:
            s.wait()
        rm[cycle, 0] += quarter[cycle, 1, 0]
        rm[cycle, 1] += qown[cycle, 1]
        rm[cycle, 2] += quarter[cycle, 0, 0]
        rm[cycle, 3] += quarter[cycle, 0, 1]
        rm[cycle, 4] += qown[cycle, 0]
        rm[cycle, 5] += quarter[cycle, 1, 1]
        for q in range(6):
            ea[q + 1] = cm[q] * rm[cycle, q]

        def mid_relax(dst, src, m):
            x = src[m + 3]
            nb = y_sides(x) + z_sides(x) + src[m + 2] + src[m + 4]
            dst[m + 3] = KEEP * x + cm[m + 2] * (rm[cycle, m + 2] + 0.25 * nb)

        for m in range(-1, 3):
            mid_relax(e2.at[cycle], ea, m)
        total = 0.0
        for m in range(2):
            x = e2[cycle, m + 3]
            nb = y_sides(x) + z_sides(x) + e2[cycle, m + 2] + e2[cycle, m + 4]
            total += rm[cycle, m + 2] - DAMPING / cm[m + 2] * x + 0.25 * nb
        gr[cycle, me] = 0.125 * sum_mid(total)
        gather_start(cycle, gr.at[cycle])
        wide = [Transfer(e2.at[cycle, a], e2.at[cycle, b], dist).start()
                for a, b, dist in ((3, 1, 1), (4, 6, -1), (4, 0, 2), (3, 7, -2))]
        both = share(v)
        if cycle == 0:
            gather_wait(CYCLES, gc)
        gather_wait(cycle, gr.at[cycle])

        def begin(q, _):
            g = gc[q] * gr[cycle, q]
            gr[CYCLES, q] = g
            xa[q + 2] = g
            return 0

        lax.fori_loop(0, n, begin, 0)

        def twice(_, c):
            coarse_sweep(xb, xa)
            coarse_sweep(xa, xb)
            return c

        lax.fori_loop(0, (COARSE - 1) // 2, twice, 0)
        coarse_sweep(xb, xa)

        for t in wide + both:
            t.wait()
        for j in range(5):
            e = spread_mid(xb[me + j])
            for m in (2 * (j - 2), 2 * (j - 2) + 1):
                if -3 <= m <= 4:
                    ea[m + 3] = e2[cycle, m + 3] + e
        for m in range(-2, 4):
            mid_relax(eb, ea, m)
        for m in range(-1, 3):
            mid_relax(ea, eb, m)
        for m in range(-1, 3):
            e = spread_fine(ea[m + 3])
            for p in (2 * m, 2 * m + 1):
                v[p + 2, rows, :] += e

    relax(vb, va, (1, 2))
    for t in first:
        t.wait()
    prepare((-1, 4))
    relax(vb, va, (0, 3))
    vcycle(0, vb)
    relax(va, vb, (-1, 0, 1))
    relax(va, vb, (2, 3, 4))
    relax(vd, va, (0, 1))
    relax(vd, va, (2, 3))
    shared = share(vd)
    relax(va, vd, (1, 2))
    for t in shared:
        t.wait()
    relax(va, vd, (0, 3))
    relax(va, vd, (-1, 4))
    relax(ve, va, (0, 3))
    relax(ve, va, (1, 2))
    vcycle(1, ve)
    relax(va, ve, (0, 1))
    beyond = Transfer(va.at[pl.ds(3, 1), rows, :], last, -1).start()
    relax(va, ve, (-1, 2))
    relax(va, ve, (3, 4))
    relax(out_ref, va, (0, 1), raw=True)
    relax(out_ref, va, (2, 3), raw=True)
    beyond.wait()

    def body(r):
        at = pl.ds(r, CHUNK)
        x, nb = neighbours(va, 4, r, None, last)
        ahead_ref[0, at, :] = KEEP * x + c_ref[5, at, :] * (f_ref[5, at, :] + nb)

    chunks(body)


def shards(n, cotangent, counts):
    nx, ny, nz = cotangent.shape
    f32 = jnp.float32
    my, mz = ny // 2, nz // 2
    cy, cz = my // 4, mz
    vmem = pl.BlockSpec(memory_space=pltpu.VMEM)
    anywhere = pl.BlockSpec(memory_space=pl.ANY)
    multiplier, following = pl.pallas_call(
        functools.partial(kernel, n),
        out_shape=(jax.ShapeDtypeStruct((nx, ny, nz), f32), jax.ShapeDtypeStruct((1, ny, nz), f32)),
        in_specs=[anywhere, anywhere],
        out_specs=(vmem, vmem),
        scratch_shapes=[
            pltpu.VMEM((nx + 2, ny, nz), f32),
            pltpu.VMEM((nx + 2, ny, nz), jnp.int32),
            pltpu.VMEM((nx + 4, ny + 2 * PAD, nz), f32),
            pltpu.VMEM((nx + 4, ny + 2 * PAD, nz), f32),
            pltpu.VMEM((nx + 4, ny + 2 * PAD, nz), f32),
            pltpu.VMEM((nx + 4, ny + 2 * PAD, nz), f32),
            pltpu.VMEM((nx + 2, ny, nz), f32),
            pltpu.VMEM((nx, ny, nz), f32),
            pltpu.VMEM((1, ny, nz), f32),
            pltpu.VMEM((CYCLES, 2, 2, my, mz), f32),
            pltpu.VMEM((2, ny, nz), f32),
            pltpu.VMEM((6, my, mz), f32),
            pltpu.VMEM((CYCLES, 6, my, mz), f32),
            pltpu.VMEM((CYCLES, 8, my, mz), f32),
            pltpu.VMEM((8, my, mz), f32),
            pltpu.VMEM((8, my, mz), f32),
            pltpu.VMEM((CYCLES, 2, my, mz), f32),
            pltpu.VMEM((n, cy, cz), f32),
            pltpu.VMEM((CYCLES + 1, n, cy, cz), f32),
            pltpu.VMEM((n + 4, cy, cz), f32),
            pltpu.VMEM((n + 4, cy, cz), f32),
            pltpu.SemaphoreType.DMA((2,)),
            pltpu.SemaphoreType.DMA((40,)),
            pltpu.SemaphoreType.DMA((40,)),
            pltpu.SemaphoreType.DMA((CYCLES + 1, n)),
            pltpu.SemaphoreType.DMA((CYCLES + 1, n)),
        ],
        compiler_params=pltpu.CompilerParams(
            collective_id=0, has_side_effects=True, vmem_limit_bytes=40 * 1024 * 1024),
    )(cotangent, counts)
    ahead_x = jnp.concatenate([multiplier[1:], following], axis=0)
    ahead_y = jnp.pad(multiplier[:, 1:], ((0, 0), (0, 1), (0, 0)))
    ahead_z = jnp.pad(multiplier[:, :, 1:], ((0, 0), (0, 0), (0, 1)))
    normal_grad = jnp.stack([multiplier - ahead_x, multiplier - ahead_y, multiplier - ahead_z])
    return (multiplier, normal_grad)


def solution(mesh):
    split = P(("scene", "gx"), None, None)
    return jax.shard_map(
        functools.partial(shards, mesh.shape["gx"]),
        mesh=mesh,
        in_specs=(split, split),
        out_specs=(split, P(None, ("scene", "gx"), None, None)),
        check_vma=False,
    )
```
